32 devices in a mesh: groups: 2 (over y), dp: 4 (over x, core), tensor: 4 (over z).
Axes of the slice: x: 2, y: 2, z: 4, core: 2. Of those that a mesh axis runs over, the one named last changes fastest.
Arguments:
- attn_out: bfloat16 [4096, 8192], P(('groups', 'dp'), 'tensor'), parts along dimension 0, may hold values from -0.75 to 0.75
- out_grad: bfloat16 [4096, 8192], P(('groups', 'dp'), 'tensor'), parts along dimension 0, may hold values from -6 to 6
- base_weight: bfloat16 [8192, 8192], P('tensor', 'dp'), may hold values from -0.0625 to 0.0625
- delta_values: bfloat16 [128, 128, 128], P('tensor'), may hold values from -0.1796875 to 0.1796875
- block_rows: int32 [128], P('tensor'), may hold values from 0 to 63, as said below
- block_cols: int32 [128], P('tensor'), may hold values from 0 to 63
- block_owner: int32 [128], P('tensor'), may hold values from 0 to 3, as said below
Outputs:
- in_grad: bfloat16 [4096, 8192], P(('groups', 'dp'), 'tensor'), parts along dimension 0
- delta_grad: float32 [8, 32, 128, 128], P(('groups', 'tensor'), 'dp'), parts along dimension 0
The draws below stay inside these ranges and needn't reach their ends.
There are 2 independent parts, one for each index of `groups`. The reference program is written for one: setup_inputs(seed, part) draws one part's arguments, and reference() takes and returns one part's arrays. A program takes and returns all parts, laid end to end along the dimension named above; an argument that names none is the same for every part. Nothing has to cross between parts.
Inputs may be any that keep to these rules, and one draw needn't show every extreme that they name: `block_rows`: piece k (entries k * 32 to k * 32 + 31) names block rows k * 16 to (k + 1) * 16 - 1; no two entries name the same block. `block_owner`: in every piece of 32 entries no owner appears more than 8 times, and some owner exactly 8 times.
All inputs are finite; a program needn't handle non-finite values.
Results may differ from the reference program's by a relative error of at most 0.0032.
Values may be sent and summed in bfloat16 or wider, within the bound.
A program may use at most 192 MiB of HBM per device.

```python
import jax
import jax.numpy as jnp
from jax import lax

D = 8192
BS = 128
TOKENS = 2048
BPT = 32
NBLK = 128
CAP = 8
N_DP = 4
N_TENSOR = 4


def shared_cells(key):
    row_span = D // N_TENSOR // BS
    col_span = D // BS
    keys = jax.random.split(key, N_TENSOR)

    def one_piece(piece_key):
        return jax.random.permutation(piece_key, row_span * col_span)[:BPT]
    cells = jax.vmap(one_piece)(keys).astype(jnp.int32)
    return (cells, row_span, col_span)


def draw_block_rows(key, part):
    cells, row_span, col_span = shared_cells(key)
    start = jnp.arange(N_TENSOR, dtype=jnp.int32)[:, None] * row_span
    return (start + cells // col_span).reshape(-1).astype(jnp.int32)


def draw_block_cols(key, part):
    cells, row_span, col_span = shared_cells(key)
    return (cells % col_span).reshape(-1).astype(jnp.int32)


def draw_block_owner(key, part):
    key = jax.random.fold_in(key, 3)
    keys = jax.random.split(key, N_TENSOR)

    def one_piece(piece_key):
        first, second, third = jax.random.split(piece_key, 3)
        busiest = jax.random.randint(first, (), 0, N_DP, dtype=jnp.int32)
        others = jax.random.permutation(second, (N_DP - 1) * CAP)[:BPT - CAP].astype(jnp.int32) // CAP
        others = others + (others >= busiest).astype(jnp.int32)
        owners = jnp.concatenate([jnp.full((CAP,), busiest, jnp.int32), others])
        return owners[jax.random.permutation(third, BPT)]
    return jax.vmap(one_piece)(keys).reshape(-1).astype(jnp.int32)


def block_levels(own_key, extent, pieces, low, largest):
    def one(axis_at, shards_of):
        heights = jax.random.uniform(jax.random.fold_in(jax.random.fold_in(own_key, 6), axis_at), (shards_of,), jnp.float32, low / len(pieces), largest / len(pieces))
        return jnp.repeat(jnp.exp(heights), extent[axis_at] // shards_of).reshape((-1,) + (1,) * (len(extent) - axis_at - 1))

    factor_of = one(*pieces[0])
    for cut in pieces[1:]:
        factor_of = factor_of * one(*cut)
    return factor_of


def normal_values(key, dims, scale, reach, cuts=(), kind=jnp.bfloat16):
    values = jax.random.normal(key, dims, jnp.float32) * scale
    if len(cuts) > 0:
        values = block_levels(key, dims, cuts, -0.22, 0.18) * values
    return jnp.clip(values, min=-reach, max=reach).astype(kind)


def setup_inputs(seed: int = 0, part: int = 0) -> dict:
    streams_of = jax.random.split(jax.random.key(seed), 8)
    part_splits = jax.random.split(jax.random.fold_in(streams_of[7], part), 8)
    return {
        "attn_out": normal_values(part_splits[0], (TOKENS, D), 0.125, 0.75, ((0, 4), (1, 4))),
        "out_grad": normal_values(part_splits[1], (TOKENS, D), 1.0, 6.0, ((0, 4), (1, 4))),
        "base_weight": normal_values(streams_of[2], (D, D), D ** -0.5, 0.0625, ((0, 4), (1, 4))),
        "delta_values": normal_values(streams_of[3], (NBLK, BS, BS), 0.03, 0.1796875, ((0, 4),)),
        "block_rows": draw_block_rows(jax.random.fold_in(streams_of[7], 71), part),
        "block_cols": draw_block_cols(jax.random.fold_in(streams_of[7], 71), part),
        "block_owner": draw_block_owner(jax.random.fold_in(streams_of[7], 71), part),
    }


def reference(attn_out, out_grad, base_weight, delta_values, block_rows, block_cols, block_owner):
    blocks = D // BS
    grid = base_weight.astype(jnp.float32).reshape(blocks, BS, blocks, BS)
    grid = grid.at[block_rows, :, block_cols, :].add(delta_values.astype(jnp.float32))
    w_eff = grid.reshape(D, D).astype(jnp.bfloat16)
    in_grad = jnp.dot(out_grad, w_eff.T, preferred_element_type=jnp.float32).astype(jnp.bfloat16)

    def one_block(pair):
        row_block, col_block = pair
        left = lax.dynamic_slice_in_dim(attn_out, (row_block * BS).astype(jnp.int32), BS, 1)
        right = lax.dynamic_slice_in_dim(out_grad, (col_block * BS).astype(jnp.int32), BS, 1)
        return jnp.dot(left.T, right, preferred_element_type=jnp.float32)

    block_grad = lax.map(one_block, (block_rows, block_cols))
    owners = block_owner.reshape(N_TENSOR, BPT)
    same = owners[:, :, None] == owners[:, None, :]
    order = jnp.arange(BPT, dtype=jnp.int32)
    earlier = order[None, :, None] > order[None, None, :]
    slot = jnp.sum((same & earlier).astype(jnp.int32), axis=2).astype(jnp.int32)
    target = owners * CAP + slot
    places = jnp.arange(N_DP * CAP, dtype=jnp.int32)
    picker = (target[:, :, None] == places[None, None, :]).astype(jnp.float32)
    delta_grad = jnp.einsum("kbs,kbrc->ksrc", picker, block_grad.reshape(N_TENSOR, BPT, BS, BS), precision=lax.Precision.HIGHEST)
    return in_grad, delta_grad
```

```python
import jax
import jax.numpy as jnp
from jax import lax
from jax.experimental import pallas as pl
from jax.experimental.pallas import tpu as pltpu
from jax.sharding import PartitionSpec as P

D = 8192
BS = 128


def per_device(attn_out, out_grad, base_weight, delta_values, block_rows, block_cols, block_owner):
    tok_rows = attn_out.shape[0]
    feat_dev = attn_out.shape[1]
    row_span = feat_dev // BS
    col_span = base_weight.shape[1] // BS
    all_cols = D // BS
    dp_count = lax.axis_size("dp")
    dp_index = lax.axis_index("dp")
    piece_len = block_owner.shape[0]
    slot_cap = max(2, (piece_len + dp_count - 1) // dp_count)
    local_rows = block_rows % row_span
    local_cols = block_cols - dp_index * col_span
    row_pick = (local_rows[:, None] == jnp.arange(row_span, dtype=jnp.int32)[None, :]).astype(
        jnp.float32
    )
    col_pick = (local_cols[:, None] == jnp.arange(col_span, dtype=jnp.int32)[None, :]).astype(
        jnp.float32
    )
    added = jnp.einsum(
        "bx,by,brc->xryc",
        row_pick,
        col_pick,
        delta_values.astype(jnp.float32),
        precision=lax.Precision.HIGHEST,
    )
    w_eff = (base_weight.astype(jnp.float32) + added.reshape(feat_dev, col_span * BS)).astype(
        jnp.bfloat16
    )
    full_grad = lax.all_gather(out_grad, "tensor", axis=1, tiled=True)
    summed = lax.dot_general(
        full_grad,
        lax.all_gather(w_eff, "dp", axis=1, tiled=True),
        (((1,), (1,)), ((), ())),
        preferred_element_type=jnp.float32,
    )
    in_grad = summed.astype(jnp.bfloat16)
    left_sel = jnp.take(attn_out.reshape(tok_rows, row_span, BS), local_rows, axis=1)
    right_sel = jnp.take(full_grad.reshape(tok_rows, all_cols, BS), block_cols, axis=1)
    partial_blocks = jnp.einsum(
        "tbr,tbc->brc", left_sel, right_sel, preferred_element_type=jnp.float32
    )
    order = jnp.arange(piece_len, dtype=jnp.int32)
    same = block_owner[:, None] == block_owner[None, :]
    earlier = order[:, None] > order[None, :]
    slot = jnp.sum((same & earlier).astype(jnp.int32), axis=1)
    target = block_owner * slot_cap + slot
    places = jnp.arange(dp_count * slot_cap, dtype=jnp.int32)
    picker = (target[:, None] == places[None, :]).astype(jnp.float32)
    packed = jnp.einsum("bs,brc->src", picker, partial_blocks, precision=lax.Precision.HIGHEST)
    packed = packed.reshape(dp_count, slot_cap, BS, BS)
    received = lax.all_to_all(packed, "dp", split_axis=0, concat_axis=0, tiled=True)
    owned = jnp.sum(received, axis=0)
    return (in_grad, owned[None])


def build_tables(block_rows, block_cols, block_owner, row_span, col_span, dp_index, dp_count, slot_cap):
    piece_len = block_owner.shape[0]
    order = jnp.arange(piece_len, dtype=jnp.int32)
    local_rows = block_rows % row_span
    local_cols = block_cols - dp_index * col_span
    cell = jnp.where(
        (local_cols >= 0) & (local_cols < col_span), local_rows * col_span + local_cols, -1
    )
    cells = jnp.arange(row_span * col_span, dtype=jnp.int32)
    here = cell[None, :] == cells[:, None]
    entry_at = jnp.sum(jnp.where(here, order[None, :], 0), axis=1, dtype=jnp.int32)
    entry_on = jnp.sum(here.astype(jnp.float32), axis=1)
    same = block_owner[:, None] == block_owner[None, :]
    earlier = order[:, None] > order[None, :]
    slot = jnp.sum((same & earlier).astype(jnp.int32), axis=1)
    target = block_owner * slot_cap + slot
    places = jnp.arange(dp_count * slot_cap, dtype=jnp.int32)
    there = target[None, :] == places[:, None]
    facts = jnp.stack([local_rows, block_cols])
    placed = jnp.sum(jnp.where(there[None], facts[:, None, :], 0), axis=2, dtype=jnp.int32)
    placed_on = jnp.sum(there.astype(jnp.float32), axis=1)
    return entry_at, entry_on, placed, placed_on


N_DP = 4
N_T = 4
SLOTS = 8
TOK = 512
WID = 2048
SPAN = WID // BS
GCH = 4
GBLK = SPAN // GCH
WCH = 8
HALF = WCH // 2
WROWS = WID // WCH
NT = 256
MESH_ID = pl.DeviceIdType.MESH


def fused(
    entry_ref, entry_on_ref, placed_ref, placed_on_ref, attn_hbm, grad_hbm, base_hbm, delta_hbm, out_hbm, dgrad_hbm,
    w_all, g_all, acc, stage, attn, attn_t, delta, dsend, drecv,
    g_send, g_recv, w_send, w_recv, d_send, d_recv, loc,
):
    grp = lax.axis_index("groups")
    me = lax.axis_index("dp")
    t = lax.axis_index("tensor")
    core = me % 2
    mate = me + 1 - 2 * core
    far = (me + 2) % 4
    far_mate = (mate + 2) % 4

    barrier = pltpu.get_barrier_semaphore()
    for step in (1, 2, 3):
        pl.semaphore_signal(
            barrier, inc=1, device_id={"dp": (me + step) % 4}, device_id_type=MESH_ID
        )
    pl.semaphore_signal(barrier, inc=1, device_id={"groups": 1 - grp}, device_id_type=MESH_ID)

    @pl.when(t > 0)
    def _():
        pl.semaphore_signal(barrier, inc=1, device_id={"tensor": t - 1}, device_id_type=MESH_ID)

    @pl.when(t < N_T - 1)
    def _():
        pl.semaphore_signal(barrier, inc=1, device_id={"tensor": t + 1}, device_id_type=MESH_ID)

    def base_copy(ch):
        rows = pl.ds(pl.multiple_of(ch * WROWS, WROWS), WROWS)
        return pltpu.make_async_copy(base_hbm.at[rows], w_all.at[me, rows], loc.at[ch])

    def own_grad(b):
        cols = pl.ds(b * BS, BS)
        return pltpu.make_async_copy(
            grad_hbm.at[:, cols], g_all.at[t * SPAN + b], loc.at[WCH + 3 + b]
        )

    attn_copy = pltpu.make_async_copy(attn_hbm, attn, loc.at[WCH + 1])
    delta_copy = pltpu.make_async_copy(delta_hbm, delta, loc.at[WCH + 2])
    for b in range(SPAN):
        own_grad(b).start()
    delta_copy.start()
    for i in range(WCH):
        base_copy((HALF * grp + i) % WCH).start()
    attn_copy.start()

    last = N_T - 1
    pl.semaphore_wait(barrier, 4 + (t + last - 1) // last + (2 * last - 1 - t) // last)

    def g_copy(shard, ch, side):
        part = g_all.at[pl.ds(shard * SPAN + ch * GBLK, GBLK)]
        return pltpu.make_async_remote_copy(
            src_ref=part,
            dst_ref=part,
            send_sem=g_send.at[side, shard, ch],
            recv_sem=g_recv.at[shard, ch],
            device_id={"tensor": t - 1 if side == 0 else t + 1},
            device_id_type=MESH_ID,
        )

    for ch in range(GCH):
        for b in range(GBLK):
            own_grad(ch * GBLK + b).wait()

        @pl.when(t > 0)
        def _():
            g_copy(t, ch, 0).start()

        @pl.when(t < N_T - 1)
        def _():
            g_copy(t, ch, 1).start()

    X, Y, C_OWN, C_FAR = 0, 1, 2, 3

    def w_copy(shard, ch, kind):
        rows = pl.ds(pl.multiple_of(ch * WROWS, WROWS), WROWS)
        if kind == X:
            dev = {"dp": far}
        elif kind == Y:
            dev = {"groups": 1 - grp}
        else:
            dev = {"dp": mate}
        return pltpu.make_async_remote_copy(
            src_ref=w_all.at[shard, rows],
            dst_ref=w_all.at[shard, rows],
            send_sem=w_send.at[kind, ch],
            recv_sem=w_recv.at[shard, ch],
            device_id=dev,
            device_id_type=MESH_ID,
        )

    delta_copy.wait()
    for i in range(WCH):
        ch = (HALF * grp + i) % WCH
        base_copy(ch).wait()

        def add_cell(n, carry, ch=ch):
            r, c = n // SPAN, n % SPAN
            rows = pl.ds(pl.multiple_of(ch * WROWS + r * BS, BS), BS)
            cols = pl.ds(pl.multiple_of(c * BS, BS), BS)
            at = ch * (WROWS // BS * SPAN) + n
            extra = delta[entry_ref[at]].astype(jnp.float32) * entry_on_ref[at]
            w_all[me, rows, cols] = (w_all[me, rows, cols].astype(jnp.float32) + extra).astype(
                jnp.bfloat16
            )
            return carry

        lax.fori_loop(0, WROWS // BS * SPAN, add_cell, 0)
        if i < HALF:
            w_copy(me, ch, X).start()
        w_copy(me, ch, C_OWN).start()

    attn_copy.wait()

    def flip(r, carry):
        cols = pl.ds(pl.multiple_of(r * BS, BS), BS)
        attn_t[r] = attn[:, cols].T
        return carry

    lax.fori_loop(0, SPAN, flip, 0)

    def left_in(m):
        return t - 1 - m // GCH, m % GCH

    def right_in(m):
        return t + 1 + m // GCH, m % GCH

    def take_left(m):
        shard, ch = left_in(m)

        @pl.when(shard >= 0)
        def _():
            g_copy(shard, ch, 1).wait_recv()

            @pl.when(t < N_T - 1)
            def _():
                g_copy(shard, ch, 1).start()

    def take_right(m):
        shard, ch = right_in(m)

        @pl.when(shard < N_T)
        def _():
            g_copy(shard, ch, 0).wait_recv()

            @pl.when(t > 0)
            def _():
                g_copy(shard, ch, 0).start()

    def x_in(i):
        return HALF * grp + i

    def y_in(i):
        return HALF * (1 - grp) + i

    for r in range(5):
        if r < 4:
            for m in (2 * r, 2 * r + 1):
                take_left(m)
                take_right(m)
            w_copy(far, x_in(r), X).wait_recv()
            w_copy(far, x_in(r), Y).start()
            w_copy(far, x_in(r), C_FAR).start()
        if r >= 1:
            w_copy(far, y_in(r - 1), Y).wait_recv()
            w_copy(far, y_in(r - 1), C_FAR).start()

    for ch in range(WCH):
        w_copy(mate, ch, C_OWN).wait_recv()
    for ch in range(WCH):
        w_copy(far_mate, ch, C_FAR).wait_recv()

    def multiply(shard, first, last):
        def tile(n, carry):
            cols = pl.ds(pl.multiple_of(n * NT, NT), NT)
            left = jnp.concatenate([g_all[shard * SPAN + b] for b in range(SPAN)], axis=1)
            part = lax.dot_general(
                left, w_all[shard, cols, :], (((1,), (1,)), ((), ())),
                preferred_element_type=jnp.float32,
            )
            if first:
                acc[:, cols] = part
            elif last:
                stage[:, cols] = (acc[:, cols] + part).astype(jnp.bfloat16)
            else:
                acc[:, cols] += part
            return carry

        lax.fori_loop(0, WID // NT, tile, 0)

    away = jnp.where(t < N_T // 2, N_T - 1, 0)
    toward = jnp.where(t < N_T // 2, 1, -1)
    multiply((away + toward) % N_T, True, False)
    multiply((away + 2 * toward) % N_T, False, False)
    multiply((away + 3 * toward) % N_T, False, False)
    for m in range(2 * GCH, 3 * GCH):
        take_left(m)
        take_right(m)

    def one_place(p, carry):
        block = jnp.dot(
            attn_t[placed_ref[0, p]], g_all[placed_ref[1, p]],
            preferred_element_type=jnp.float32,
        )
        dsend[p] = block * placed_on_ref[p]
        return carry

    def d_copy(peer):
        return pltpu.make_async_remote_copy(
            src_ref=dsend.at[pl.ds(pl.multiple_of(peer * SLOTS, SLOTS), SLOTS)],
            dst_ref=drecv.at[me],
            send_sem=d_send.at[peer],
            recv_sem=d_recv.at[me],
            device_id={"dp": peer},
            device_id_type=MESH_ID,
        )

    def d_wait(peer):
        return pltpu.make_async_remote_copy(
            src_ref=dsend.at[pl.ds(pl.multiple_of(peer * SLOTS, SLOTS), SLOTS)],
            dst_ref=drecv.at[peer],
            send_sem=d_send.at[peer],
            recv_sem=d_recv.at[peer],
            device_id={"dp": peer},
            device_id_type=MESH_ID,
        )

    for peer in (far, far_mate, mate):
        lax.fori_loop(peer * SLOTS, (peer + 1) * SLOTS, one_place, 0)
        d_copy(peer).start()
    lax.fori_loop(me * SLOTS, (me + 1) * SLOTS, one_place, 0)

    multiply(away, False, True)
    out_copy = pltpu.make_async_copy(stage, out_hbm, loc.at[WCH + 3 + SPAN])
    out_copy.start()

    for peer in (mate, far, far_mate):
        d_wait(peer).wait_recv()

    def add_up(s, carry):
        drecv[me, s] = (
            dsend[me * SLOTS + s] + drecv[mate, s] + drecv[far, s] + drecv[far_mate, s]
        )
        return carry

    lax.fori_loop(0, SLOTS, add_up, 0)
    d_out = pltpu.make_async_copy(drecv.at[me], dgrad_hbm.at[0], loc.at[WCH + 4 + SPAN])
    d_out.start()

    for peer in (mate, far, far_mate):
        d_copy(peer).wait_send()
    for i in range(HALF):
        w_copy(me, HALF * grp + i, X).wait_send()
        w_copy(far, x_in(i), Y).wait_send()
    for ch in range(WCH):
        w_copy(me, ch, C_OWN).wait_send()
        w_copy(far, ch, C_FAR).wait_send()
    for shard in range(N_T):
        for ch in range(GCH):
            @pl.when((t > 0) & (shard >= t))
            def _():
                g_copy(shard, ch, 0).wait_send()

            @pl.when((t < N_T - 1) & (shard <= t))
            def _():
                g_copy(shard, ch, 1).wait_send()
    out_copy.wait()
    d_out.wait()


def per_device_fused(
    attn_out, out_grad, base_weight, delta_values, block_rows, block_cols, block_owner
):
    tables = build_tables(
        block_rows, block_cols, block_owner, SPAN, SPAN, lax.axis_index("dp"), N_DP, SLOTS
    )
    smem = pl.BlockSpec(memory_space=pltpu.SMEM)
    hbm = pl.BlockSpec(memory_space=pl.ANY)
    dma = pltpu.SemaphoreType.DMA
    return tuple(pl.pallas_call(
        fused,
        out_shape=(
            jax.ShapeDtypeStruct((TOK, WID), jnp.bfloat16),
            jax.ShapeDtypeStruct((1, SLOTS, BS, BS), jnp.float32),
        ),
        in_specs=[smem, smem, smem, smem, hbm, hbm, hbm, hbm],
        out_specs=(hbm, hbm),
        scratch_shapes=[
            pltpu.VMEM((N_DP, WID, WID), jnp.bfloat16),
            pltpu.VMEM((N_T * SPAN, TOK, BS), jnp.bfloat16),
            pltpu.VMEM((TOK, WID), jnp.float32),
            pltpu.VMEM((TOK, WID), jnp.bfloat16),
            pltpu.VMEM((TOK, WID), jnp.bfloat16),
            pltpu.VMEM((SPAN, BS, TOK), jnp.bfloat16),
            pltpu.VMEM((N_DP * SLOTS, BS, BS), jnp.bfloat16),
            pltpu.VMEM((N_DP * SLOTS, BS, BS), jnp.float32),
            pltpu.VMEM((N_DP, SLOTS, BS, BS), jnp.float32),
            dma((2, N_T, GCH)),
            dma((N_T, GCH)),
            dma((4, WCH)),
            dma((N_DP, WCH)),
            dma((N_DP,)),
            dma((N_DP,)),
            dma((WCH + 5 + SPAN,)),
        ],
        compiler_params=pltpu.CompilerParams(
            collective_id=0, has_side_effects=True, vmem_limit_bytes=60 * 1024 * 1024
        ),
        cost_estimate=pl.CostEstimate(
            flops=2 * TOK * WID * D, bytes_accessed=16 * 1024 * 1024, transcendentals=0
        ),
    )(*tables, attn_out, out_grad, base_weight, delta_values))


def solution(mesh):
    placed = (
        P(("groups", "dp"), "tensor"),
        P(("groups", "dp"), "tensor"),
        P("tensor", "dp"),
        P("tensor", None, None),
        P("tensor"),
        P("tensor"),
        P("tensor"),
    )
    here = (mesh.shape["groups"], mesh.shape["dp"], mesh.shape["tensor"])
    return jax.shard_map(
        per_device_fused if here == (2, N_DP, N_T) else per_device,
        mesh=mesh,
        in_specs=placed,
        out_specs=(P(("groups", "dp"), "tensor"), P(("groups", "tensor"), "dp", None, None)),
        check_vma=False,
    )
```

```python
import jax
import jax.numpy as jnp
from jax import lax
from jax.experimental import pallas as pl
from jax.experimental.pallas import tpu as pltpu
from jax.sharding import PartitionSpec as P

D = 8192
BS = 128


def per_device(attn_out, out_grad, base_weight, delta_values, block_rows, block_cols, block_owner):
    tok_rows = attn_out.shape[0]
    feat_dev = attn_out.shape[1]
    row_span = feat_dev // BS
    col_span = base_weight.shape[1] // BS
    all_cols = D // BS
    dp_count = lax.axis_size("dp")
    dp_index = lax.axis_index("dp")
    piece_len = block_owner.shape[0]
    slot_cap = max(2, (piece_len + dp_count - 1) // dp_count)
    local_rows = block_rows % row_span
    local_cols = block_cols - dp_index * col_span
    row_pick = (local_rows[:, None] == jnp.arange(row_span, dtype=jnp.int32)[None, :]).astype(
        jnp.float32
    )
    col_pick = (local_cols[:, None] == jnp.arange(col_span, dtype=jnp.int32)[None, :]).astype(
        jnp.float32
    )
    added = jnp.einsum(
        "bx,by,brc->xryc",
        row_pick,
        col_pick,
        delta_values.astype(jnp.float32),
        precision=lax.Precision.HIGHEST,
    )
    w_eff = (base_weight.astype(jnp.float32) + added.reshape(feat_dev, col_span * BS)).astype(
        jnp.bfloat16
    )
    full_grad = lax.all_gather(out_grad, "tensor", axis=1, tiled=True)
    summed = lax.dot_general(
        full_grad,
        lax.all_gather(w_eff, "dp", axis=1, tiled=True),
        (((1,), (1,)), ((), ())),
        preferred_element_type=jnp.float32,
    )
    in_grad = summed.astype(jnp.bfloat16)
    left_sel = jnp.take(attn_out.reshape(tok_rows, row_span, BS), local_rows, axis=1)
    right_sel = jnp.take(full_grad.reshape(tok_rows, all_cols, BS), block_cols, axis=1)
    partial_blocks = jnp.einsum(
        "tbr,tbc->brc", left_sel, right_sel, preferred_element_type=jnp.float32
    )
    order = jnp.arange(piece_len, dtype=jnp.int32)
    same = block_owner[:, None] == block_owner[None, :]
    earlier = order[:, None] > order[None, :]
    slot = jnp.sum((same & earlier).astype(jnp.int32), axis=1)
    target = block_owner * slot_cap + slot
    places = jnp.arange(dp_count * slot_cap, dtype=jnp.int32)
    picker = (target[:, None] == places[None, :]).astype(jnp.float32)
    packed = jnp.einsum("bs,brc->src", picker, partial_blocks, precision=lax.Precision.HIGHEST)
    packed = packed.reshape(dp_count, slot_cap, BS, BS)
    received = lax.all_to_all(packed, "dp", split_axis=0, concat_axis=0, tiled=True)
    owned = jnp.sum(received, axis=0)
    return (in_grad, owned[None])


N_DP = 4
N_T = 4
SLOTS = 8
TOK = 512
WID = 2048
SPAN = WID // BS
GCH = 4
GBLK = SPAN // GCH
WCH = 8
HALF = WCH // 2
WROWS = WID // WCH
NT = 256
MESH_ID = pl.DeviceIdType.MESH


def fused(
    rows_ref, cols_ref, owner_ref, attn_hbm, grad_hbm, base_hbm, delta_hbm, out_hbm, dgrad_hbm,
    w_all, g_all, acc, stage, attn, attn_t, delta, dsend, core_in,
    chip_sum, far_in, made, entry_ref, placed_ref,
    g_send, g_recv, w_send, w_recv, d_send, d_recv, loc,
):
    grp = lax.axis_index("groups")
    me = lax.axis_index("dp")
    t = lax.axis_index("tensor")
    core = me % 2
    mate = me + 1 - 2 * core
    far = (me + 2) % 4
    far_mate = (mate + 2) % 4

    barrier = pltpu.get_barrier_semaphore()
    for peer in (mate, far):
        pl.semaphore_signal(barrier, inc=1, device_id={"dp": peer}, device_id_type=MESH_ID)
    pl.semaphore_signal(barrier, inc=1, device_id={"groups": 1 - grp}, device_id_type=MESH_ID)

    @pl.when(t > 0)
    def _():
        pl.semaphore_signal(barrier, inc=1, device_id={"tensor": t - 1}, device_id_type=MESH_ID)

    @pl.when(t < N_T - 1)
    def _():
        pl.semaphore_signal(barrier, inc=1, device_id={"tensor": t + 1}, device_id_type=MESH_ID)

    def base_copy(ch):
        rows = pl.ds(pl.multiple_of(ch * WROWS, WROWS), WROWS)
        return pltpu.make_async_copy(base_hbm.at[rows], w_all.at[me, rows], loc.at[ch])

    def own_grad(b):
        cols = pl.ds(b * BS, BS)
        return pltpu.make_async_copy(
            grad_hbm.at[:, cols], g_all.at[t * SPAN + b], loc.at[WCH + 3 + b]
        )

    attn_copy = pltpu.make_async_copy(attn_hbm, attn, loc.at[WCH + 1])
    delta_copy = pltpu.make_async_copy(delta_hbm, delta, loc.at[WCH + 2])
    for b in range(SPAN):
        own_grad(b).start()
    delta_copy.start()
    for i in range(WCH):
        base_copy((HALF * grp + i) % WCH).start()
    attn_copy.start()

    last = N_T - 1
    pl.semaphore_wait(barrier, 3 + (t + last - 1) // last + (2 * last - 1 - t) // last)

    def g_copy(shard, ch, side):
        part = g_all.at[pl.ds(shard * SPAN + ch * GBLK, GBLK)]
        return pltpu.make_async_remote_copy(
            src_ref=part,
            dst_ref=part,
            send_sem=g_send.at[side, shard, ch],
            recv_sem=g_recv.at[shard, ch],
            device_id={"tensor": t - 1 if side == 0 else t + 1},
            device_id_type=MESH_ID,
        )

    for ch in range(GCH):
        for b in range(GBLK):
            own_grad(ch * GBLK + b).wait()

        @pl.when(t > 0)
        def _():
            g_copy(t, ch, 0).start()

        @pl.when(t < N_T - 1)
        def _():
            g_copy(t, ch, 1).start()

    X, Y, C_OWN, C_FAR = 0, 1, 2, 3

    def w_copy(shard, ch, kind):
        rows = pl.ds(pl.multiple_of(ch * WROWS, WROWS), WROWS)
        if kind == X:
            dev = {"dp": far}
        elif kind == Y:
            dev = {"groups": 1 - grp}
        else:
            dev = {"dp": mate}
        return pltpu.make_async_remote_copy(
            src_ref=w_all.at[shard, rows],
            dst_ref=w_all.at[shard, rows],
            send_sem=w_send.at[kind, ch],
            recv_sem=w_recv.at[shard, ch],
            device_id=dev,
            device_id_type=MESH_ID,
        )

    cell_row = lax.broadcasted_iota(jnp.int32, (SPAN, BS), 0)
    cell_col = lax.broadcasted_iota(jnp.int32, (SPAN, BS), 1) + me * SPAN
    place = lax.broadcasted_iota(jnp.int32, (SPAN, BS), 1)
    place_owner, place_slot = place >> 3, place & (SLOTS - 1)
    zero = jnp.zeros((SPAN, BS), jnp.int32)
    entry, entry_on, seen, row_at, col_at, on_at = zero, zero, zero, zero, zero, zero
    for n in range(rows_ref.shape[0]):
        row, col, owner = rows_ref[n] & (SPAN - 1), cols_ref[n], owner_ref[n]
        hit = (cell_row == row) & (cell_col == col)
        entry = jnp.where(hit, n, entry)
        entry_on = jnp.where(hit, 1, entry_on)
        mine = place_owner == owner
        fits = mine & (place_slot == seen)
        row_at = jnp.where(fits, row, row_at)
        col_at = jnp.where(fits, col, col_at)
        on_at = jnp.where(fits, 1, on_at)
        seen = jnp.where(mine, seen + 1, seen)
    for n, table in enumerate((entry, entry_on, row_at, col_at, on_at)):
        made[n] = table
    entry_copy = pltpu.make_async_copy(made.at[pl.ds(0, 2)], entry_ref, loc.at[WCH + 5 + SPAN])
    placed_copy = pltpu.make_async_copy(made.at[pl.ds(2, 3)], placed_ref, loc.at[WCH + 6 + SPAN])
    entry_copy.start()
    placed_copy.start()
    entry_copy.wait()
    placed_copy.wait()

    delta_copy.wait()
    for i in range(WCH):
        ch = (HALF * grp + i) % WCH
        base_copy(ch).wait()

        def add_cell(n, carry, ch=ch):
            r, c = n // SPAN, n % SPAN
            rows = pl.ds(pl.multiple_of(ch * WROWS + r * BS, BS), BS)
            cols = pl.ds(pl.multiple_of(c * BS, BS), BS)
            at = ch * (WROWS // BS) + r
            extra = delta[entry_ref[0, at, c]].astype(jnp.float32)
            extra = extra * entry_ref[1, at, c].astype(jnp.float32)
            w_all[me, rows, cols] = (w_all[me, rows, cols].astype(jnp.float32) + extra).astype(
                jnp.bfloat16
            )
            return carry

        lax.fori_loop(0, WROWS // BS * SPAN, add_cell, 0)
        if i < HALF:
            w_copy(me, ch, X).start()
        w_copy(me, ch, C_OWN).start()

    attn_copy.wait()

    def flip(r, carry):
        cols = pl.ds(pl.multiple_of(r * BS, BS), BS)
        attn_t[r] = attn[:, cols].T
        return carry

    lax.fori_loop(0, SPAN, flip, 0)

    def left_in(m):
        return t - 1 - m // GCH, m % GCH

    def right_in(m):
        return t + 1 + m // GCH, m % GCH

    def take_left(m):
        shard, ch = left_in(m)

        @pl.when(shard >= 0)
        def _():
            g_copy(shard, ch, 1).wait_recv()

            @pl.when(t < N_T - 1)
            def _():
                g_copy(shard, ch, 1).start()

    def take_right(m):
        shard, ch = right_in(m)

        @pl.when(shard < N_T)
        def _():
            g_copy(shard, ch, 0).wait_recv()

            @pl.when(t > 0)
            def _():
                g_copy(shard, ch, 0).start()

    def x_in(i):
        return HALF * grp + i

    def y_in(i):
        return HALF * (1 - grp) + i

    for r in range(5):
        if r < 4:
            for m in (2 * r, 2 * r + 1):
                take_left(m)
                take_right(m)
            w_copy(far, x_in(r), X).wait_recv()
            w_copy(far, x_in(r), Y).start()
            w_copy(far, x_in(r), C_FAR).start()
        if r >= 1:
            w_copy(far, y_in(r - 1), Y).wait_recv()
            w_copy(far, y_in(r - 1), C_FAR).start()

    for ch in range(WCH):
        w_copy(mate, ch, C_OWN).wait_recv()
    for ch in range(WCH):
        w_copy(far_mate, ch, C_FAR).wait_recv()

    def multiply(shard, first, last):
        def tile(n, carry):
            cols = pl.ds(pl.multiple_of(n * NT, NT), NT)
            left = jnp.concatenate([g_all[shard * SPAN + b] for b in range(SPAN)], axis=1)
            part = lax.dot_general(
                left, w_all[shard, cols, :], (((1,), (1,)), ((), ())),
                preferred_element_type=jnp.float32,
            )
            if first:
                acc[:, cols] = part
            elif last:
                stage[:, cols] = (acc[:, cols] + part).astype(jnp.bfloat16)
            else:
                acc[:, cols] += part
            return carry

        lax.fori_loop(0, WID // NT, tile, 0)

    away = jnp.where(t < N_T // 2, N_T - 1, 0)
    toward = jnp.where(t < N_T // 2, 1, -1)
    multiply((away + toward) % N_T, True, False)
    multiply((away + 2 * toward) % N_T, False, False)
    multiply((away + 3 * toward) % N_T, False, False)
    for m in range(2 * GCH, 3 * GCH):
        take_left(m)
        take_right(m)

    def fill(peer):
        def one_place(n, carry):
            p = peer * SLOTS + n
            block = jnp.dot(
                attn_t[placed_ref[0, 0, p]], g_all[placed_ref[1, 0, p]],
                preferred_element_type=jnp.float32,
            )
            dsend[p] = block * placed_ref[2, 0, p].astype(jnp.float32)
            return carry

        lax.fori_loop(0, SLOTS, one_place, 0, unroll=4)

    def slots_of(peer):
        return pl.ds(pl.multiple_of(peer * SLOTS, SLOTS), SLOTS)

    def core_copy(side):
        return pltpu.make_async_remote_copy(
            src_ref=dsend.at[slots_of(far_mate if side == 0 else mate)],
            dst_ref=core_in.at[side],
            send_sem=d_send.at[side],
            recv_sem=d_recv.at[side],
            device_id={"dp": mate},
            device_id_type=MESH_ID,
        )

    def far_copy():
        return pltpu.make_async_remote_copy(
            src_ref=chip_sum,
            dst_ref=far_in,
            send_sem=d_send.at[2],
            recv_sem=d_recv.at[2],
            device_id={"dp": far},
            device_id_type=MESH_ID,
        )

    fill(far_mate)
    core_copy(0).start()
    fill(far)
    core_copy(0).wait_recv()

    def chip_add(n, carry):
        chip_sum[n] = (dsend[far * SLOTS + n] + core_in[0, n]).astype(jnp.bfloat16)
        return carry

    lax.fori_loop(0, SLOTS, chip_add, 0)
    far_copy().start()
    fill(mate)
    core_copy(1).start()
    fill(me)

    multiply(away, False, True)
    out_copy = pltpu.make_async_copy(stage, out_hbm, loc.at[WCH + 3 + SPAN])
    out_copy.start()

    core_copy(1).wait_recv()
    far_copy().wait_recv()

    def add_up(n, carry):
        p = me * SLOTS + n
        dsend[p] = dsend[p] + core_in[1, n] + far_in[n].astype(jnp.float32)
        return carry

    lax.fori_loop(0, SLOTS, add_up, 0)
    d_out = pltpu.make_async_copy(
        dsend.at[slots_of(me)], dgrad_hbm.at[0], loc.at[WCH + 4 + SPAN]
    )
    d_out.start()

    core_copy(0).wait_send()
    core_copy(1).wait_send()
    far_copy().wait_send()
    for i in range(HALF):
        w_copy(me, HALF * grp + i, X).wait_send()
        w_copy(far, x_in(i), Y).wait_send()
    for ch in range(WCH):
        w_copy(me, ch, C_OWN).wait_send()
        w_copy(far, ch, C_FAR).wait_send()
    for shard in range(N_T):
        for ch in range(GCH):
            @pl.when((t > 0) & (shard >= t))
            def _():
                g_copy(shard, ch, 0).wait_send()

            @pl.when((t < N_T - 1) & (shard <= t))
            def _():
                g_copy(shard, ch, 1).wait_send()
    out_copy.wait()
    d_out.wait()


def per_device_fused(
    attn_out, out_grad, base_weight, delta_values, block_rows, block_cols, block_owner
):
    smem = pl.BlockSpec(memory_space=pltpu.SMEM)
    hbm = pl.BlockSpec(memory_space=pl.ANY)
    dma = pltpu.SemaphoreType.DMA
    return tuple(pl.pallas_call(
        fused,
        out_shape=(
            jax.ShapeDtypeStruct((TOK, WID), jnp.bfloat16),
            jax.ShapeDtypeStruct((1, SLOTS, BS, BS), jnp.float32),
        ),
        in_specs=[smem, smem, smem, hbm, hbm, hbm, hbm],
        out_specs=(hbm, hbm),
        scratch_shapes=[
            pltpu.VMEM((N_DP, WID, WID), jnp.bfloat16),
            pltpu.VMEM((N_T * SPAN, TOK, BS), jnp.bfloat16),
            pltpu.VMEM((TOK, WID), jnp.float32),
            pltpu.VMEM((TOK, WID), jnp.bfloat16),
            pltpu.VMEM((TOK, WID), jnp.bfloat16),
            pltpu.VMEM((SPAN, BS, TOK), jnp.bfloat16),
            pltpu.VMEM((N_DP * SLOTS, BS, BS), jnp.bfloat16),
            pltpu.VMEM((N_DP * SLOTS, BS, BS), jnp.float32),
            pltpu.VMEM((2, SLOTS, BS, BS), jnp.float32),
            pltpu.VMEM((SLOTS, BS, BS), jnp.bfloat16),
            pltpu.VMEM((SLOTS, BS, BS), jnp.bfloat16),
            pltpu.VMEM((5, SPAN, BS), jnp.int32),
            pltpu.SMEM((2, SPAN, BS), jnp.int32),
            pltpu.SMEM((3, SPAN, BS), jnp.int32),
            dma((2, N_T, GCH)),
            dma((N_T, GCH)),
            dma((4, WCH)),
            dma((N_DP, WCH)),
            dma((3,)),
            dma((3,)),
            dma((WCH + 7 + SPAN,)),
        ],
        compiler_params=pltpu.CompilerParams(
            collective_id=0, has_side_effects=True, vmem_limit_bytes=60 * 1024 * 1024
        ),
        cost_estimate=pl.CostEstimate(
            flops=2 * TOK * WID * D, bytes_accessed=16 * 1024 * 1024, transcendentals=0
        ),
    )(
        block_rows, block_cols, block_owner, attn_out, out_grad, base_weight, delta_values
    ))


def solution(mesh):
    placed = (
        P(("groups", "dp"), "tensor"),
        P(("groups", "dp"), "tensor"),
        P("tensor", "dp"),
        P("tensor", None, None),
        P("tensor"),
        P("tensor"),
        P("tensor"),
    )
    here = (mesh.shape["groups"], mesh.shape["dp"], mesh.shape["tensor"])
    return jax.shard_map(
        per_device_fused if here == (2, N_DP, N_T) else per_device,
        mesh=mesh,
        in_specs=placed,
        out_specs=(P(("groups", "dp"), "tensor"), P(("groups", "tensor"), "dp", None, None)),
        check_vma=False,
    )
```

```python
import jax
import jax.numpy as jnp
from jax import lax
from jax.experimental import pallas as pl
from jax.experimental.pallas import tpu as pltpu
from jax.sharding import PartitionSpec as P

D = 8192
BS = 128


def per_device(attn_out, out_grad, base_weight, delta_values, block_rows, block_cols, block_owner):
    tok_rows = attn_out.shape[0]
    feat_dev = attn_out.shape[1]
    row_span = feat_dev // BS
    col_span = base_weight.shape[1] // BS
    all_cols = D // BS
    dp_count = lax.axis_size("dp")
    dp_index = lax.axis_index("dp")
    piece_len = block_owner.shape[0]
    slot_cap = max(2, (piece_len + dp_count - 1) // dp_count)
    local_rows = block_rows % row_span
    local_cols = block_cols - dp_index * col_span
    row_pick = (local_rows[:, None] == jnp.arange(row_span, dtype=jnp.int32)[None, :]).astype(
        jnp.float32
    )
    col_pick = (local_cols[:, None] == jnp.arange(col_span, dtype=jnp.int32)[None, :]).astype(
        jnp.float32
    )
    added = jnp.einsum(
        "bx,by,brc->xryc",
        row_pick,
        col_pick,
        delta_values.astype(jnp.float32),
        precision=lax.Precision.HIGHEST,
    )
    w_eff = (base_weight.astype(jnp.float32) + added.reshape(feat_dev, col_span * BS)).astype(
        jnp.bfloat16
    )
    full_grad = lax.all_gather(out_grad, "tensor", axis=1, tiled=True)
    summed = lax.dot_general(
        full_grad,
        lax.all_gather(w_eff, "dp", axis=1, tiled=True),
        (((1,), (1,)), ((), ())),
        preferred_element_type=jnp.float32,
    )
    in_grad = summed.astype(jnp.bfloat16)
    left_sel = jnp.take(attn_out.reshape(tok_rows, row_span, BS), local_rows, axis=1)
    right_sel = jnp.take(full_grad.reshape(tok_rows, all_cols, BS), block_cols, axis=1)
    partial_blocks = jnp.einsum(
        "tbr,tbc->brc", left_sel, right_sel, preferred_element_type=jnp.float32
    )
    order = jnp.arange(piece_len, dtype=jnp.int32)
    same = block_owner[:, None] == block_owner[None, :]
    earlier = order[:, None] > order[None, :]
    slot = jnp.sum((same & earlier).astype(jnp.int32), axis=1)
    target = block_owner * slot_cap + slot
    places = jnp.arange(dp_count * slot_cap, dtype=jnp.int32)
    picker = (target[:, None] == places[None, :]).astype(jnp.float32)
    packed = jnp.einsum("bs,brc->src", picker, partial_blocks, precision=lax.Precision.HIGHEST)
    packed = packed.reshape(dp_count, slot_cap, BS, BS)
    received = lax.all_to_all(packed, "dp", split_axis=0, concat_axis=0, tiled=True)
    owned = jnp.sum(received, axis=0)
    return (in_grad, owned[None])


N_DP = 4
N_T = 4
SLOTS = 8
TOK = 512
WID = 2048
SPAN = WID // BS
GCH = 4
GBLK = SPAN // GCH
WCH = 8
HALF = WCH // 2
WROWS = WID // WCH
NT = 256
MESH_ID = pl.DeviceIdType.MESH


def fused(
    rows_ref, cols_ref, owner_ref, attn_hbm, grad_hbm, base_hbm, delta_hbm, out_ref, dgrad_ref,
    w_all, g_all, acc, attn, attn_t, delta, dsend, core_in,
    chip_sum, far_in, made, entry_ref, placed_ref,
    g_send, g_recv, w_send, w_recv, d_send, d_recv, loc,
):
    grp = lax.axis_index("groups")
    me = lax.axis_index("dp")
    t = lax.axis_index("tensor")
    core = me % 2
    mate = me + 1 - 2 * core
    far = (me + 2) % 4
    far_mate = (mate + 2) % 4

    barrier = pltpu.get_barrier_semaphore()
    for peer in (mate, far):
        pl.semaphore_signal(barrier, inc=1, device_id={"dp": peer}, device_id_type=MESH_ID)
    pl.semaphore_signal(barrier, inc=1, device_id={"groups": 1 - grp}, device_id_type=MESH_ID)

    @pl.when(t > 0)
    def _():
        pl.semaphore_signal(barrier, inc=1, device_id={"tensor": t - 1}, device_id_type=MESH_ID)

    @pl.when(t < N_T - 1)
    def _():
        pl.semaphore_signal(barrier, inc=1, device_id={"tensor": t + 1}, device_id_type=MESH_ID)

    def base_copy(ch):
        rows = pl.ds(pl.multiple_of(ch * WROWS, WROWS), WROWS)
        return pltpu.make_async_copy(base_hbm.at[rows], w_all.at[me, rows], loc.at[ch])

    def own_grad(b):
        cols = pl.ds(b * BS, BS)
        return pltpu.make_async_copy(
            grad_hbm.at[:, cols], g_all.at[t * SPAN + b], loc.at[WCH + 3 + b]
        )

    attn_copy = pltpu.make_async_copy(attn_hbm, attn, loc.at[WCH + 1])
    delta_copy = pltpu.make_async_copy(delta_hbm, delta, loc.at[WCH + 2])
    for b in range(SPAN):
        own_grad(b).start()
    delta_copy.start()
    for i in range(WCH):
        base_copy((HALF * grp + i) % WCH).start()
    attn_copy.start()

    last = N_T - 1
    pl.semaphore_wait(barrier, 3 + (t + last - 1) // last + (2 * last - 1 - t) // last)

    def g_copy(shard, ch, side):
        part = g_all.at[pl.ds(shard * SPAN + ch * GBLK, GBLK)]
        return pltpu.make_async_remote_copy(
            src_ref=part,
            dst_ref=part,
            send_sem=g_send.at[side, shard, ch],
            recv_sem=g_recv.at[shard, ch],
            device_id={"tensor": t - 1 if side == 0 else t + 1},
            device_id_type=MESH_ID,
        )

    for ch in range(GCH):
        for b in range(GBLK):
            own_grad(ch * GBLK + b).wait()

        @pl.when(t > 0)
        def _():
            g_copy(t, ch, 0).start()

        @pl.when(t < N_T - 1)
        def _():
            g_copy(t, ch, 1).start()

    X, Y, C_OWN, C_FAR = 0, 1, 2, 3

    def w_copy(shard, ch, kind):
        rows = pl.ds(pl.multiple_of(ch * WROWS, WROWS), WROWS)
        if kind == X:
            dev = {"dp": far}
        elif kind == Y:
            dev = {"groups": 1 - grp}
        else:
            dev = {"dp": mate}
        return pltpu.make_async_remote_copy(
            src_ref=w_all.at[shard, rows],
            dst_ref=w_all.at[shard, rows],
            send_sem=w_send.at[kind, ch],
            recv_sem=w_recv.at[shard, ch],
            device_id=dev,
            device_id_type=MESH_ID,
        )

    cell_row = lax.broadcasted_iota(jnp.int32, (SPAN, BS), 0)
    cell_col = lax.broadcasted_iota(jnp.int32, (SPAN, BS), 1) + me * SPAN
    place = lax.broadcasted_iota(jnp.int32, (SPAN, BS), 1)
    place_owner, place_slot = place >> 3, place & (SLOTS - 1)
    zero = jnp.zeros((SPAN, BS), jnp.int32)
    entry, entry_on, seen, row_at, col_at, on_at = zero, zero, zero, zero, zero, zero
    for n in range(rows_ref.shape[0]):
        row, col, owner = rows_ref[n] & (SPAN - 1), cols_ref[n], owner_ref[n]
        hit = (cell_row == row) & (cell_col == col)
        entry = jnp.where(hit, n, entry)
        entry_on = jnp.where(hit, 1, entry_on)
        mine = place_owner == owner
        fits = mine & (place_slot == seen)
        row_at = jnp.where(fits, row, row_at)
        col_at = jnp.where(fits, col, col_at)
        on_at = jnp.where(fits, 1, on_at)
        seen = jnp.where(mine, seen + 1, seen)
    for n, table in enumerate((entry, entry_on, row_at, col_at, on_at)):
        made[n] = table
    entry_copy = pltpu.make_async_copy(made.at[pl.ds(0, 2)], entry_ref, loc.at[WCH + 5 + SPAN])
    placed_copy = pltpu.make_async_copy(made.at[pl.ds(2, 3)], placed_ref, loc.at[WCH + 6 + SPAN])
    entry_copy.start()
    placed_copy.start()
    entry_copy.wait()
    placed_copy.wait()

    delta_copy.wait()
    for i in range(WCH):
        ch = (HALF * grp + i) % WCH
        base_copy(ch).wait()

        def add_cell(n, carry, ch=ch):
            r, c = n // SPAN, n % SPAN
            rows = pl.ds(pl.multiple_of(ch * WROWS + r * BS, BS), BS)
            cols = pl.ds(pl.multiple_of(c * BS, BS), BS)
            at = ch * (WROWS // BS) + r
            extra = delta[entry_ref[0, at, c]].astype(jnp.float32)
            extra = extra * entry_ref[1, at, c].astype(jnp.float32)
            w_all[me, rows, cols] = (w_all[me, rows, cols].astype(jnp.float32) + extra).astype(
                jnp.bfloat16
            )
            return carry

        lax.fori_loop(0, WROWS // BS * SPAN, add_cell, 0)
        if i < HALF:
            w_copy(me, ch, X).start()
        w_copy(me, ch, C_OWN).start()

    attn_copy.wait()

    def flip(r, carry):
        cols = pl.ds(pl.multiple_of(r * BS, BS), BS)
        attn_t[r] = attn[:, cols].T
        return carry

    lax.fori_loop(0, SPAN, flip, 0)

    def left_in(m):
        return t - 1 - m // GCH, m % GCH

    def right_in(m):
        return t + 1 + m // GCH, m % GCH

    def take_left(m):
        shard, ch = left_in(m)

        @pl.when(shard >= 0)
        def _():
            g_copy(shard, ch, 1).wait_recv()

            @pl.when(t < N_T - 1)
            def _():
                g_copy(shard, ch, 1).start()

    def take_right(m):
        shard, ch = right_in(m)

        @pl.when(shard < N_T)
        def _():
            g_copy(shard, ch, 0).wait_recv()

            @pl.when(t > 0)
            def _():
                g_copy(shard, ch, 0).start()

    def x_in(i):
        return HALF * grp + i

    def y_in(i):
        return HALF * (1 - grp) + i

    for r in range(5):
        if r < 4:
            for m in range(r * GCH // 2, (r + 1) * GCH // 2):
                take_left(m)
                take_right(m)
            w_copy(far, x_in(r), X).wait_recv()
            w_copy(far, x_in(r), Y).start()
            w_copy(far, x_in(r), C_FAR).start()
        if r >= 1:
            w_copy(far, y_in(r - 1), Y).wait_recv()
            w_copy(far, y_in(r - 1), C_FAR).start()

    for ch in range(WCH):
        w_copy(mate, ch, C_OWN).wait_recv()
    for ch in range(WCH):
        w_copy(far_mate, ch, C_FAR).wait_recv()

    def multiply(shard, first, last):
        def tile(n, carry):
            cols = pl.ds(pl.multiple_of(n * NT, NT), NT)
            left = jnp.concatenate([g_all[shard * SPAN + b] for b in range(SPAN)], axis=1)
            part = lax.dot_general(
                left, w_all[shard, cols, :], (((1,), (1,)), ((), ())),
                preferred_element_type=jnp.float32,
            )
            if first:
                acc[:, cols] = part
            elif last:
                out_ref[:, cols] = (acc[:, cols] + part).astype(jnp.bfloat16)
            else:
                acc[:, cols] += part
            return carry

        lax.fori_loop(0, WID // NT, tile, 0)

    away = jnp.where(t < N_T // 2, N_T - 1, 0)
    toward = jnp.where(t < N_T // 2, 1, -1)
    multiply((away + toward) % N_T, True, False)
    multiply((away + 2 * toward) % N_T, False, False)
    multiply((away + 3 * toward) % N_T, False, False)
    for m in range(2 * GCH, 3 * GCH):
        take_left(m)
        take_right(m)

    def fill(peer):
        def one_place(n, carry):
            p = peer * SLOTS + n
            block = jnp.dot(
                attn_t[placed_ref[0, 0, p]], g_all[placed_ref[1, 0, p]],
                preferred_element_type=jnp.float32,
            )
            dsend[p] = block * placed_ref[2, 0, p].astype(jnp.float32)
            return carry

        lax.fori_loop(0, SLOTS, one_place, 0, unroll=4)

    def slots_of(peer):
        return pl.ds(pl.multiple_of(peer * SLOTS, SLOTS), SLOTS)

    def core_copy(side):
        return pltpu.make_async_remote_copy(
            src_ref=dsend.at[slots_of(far_mate if side == 0 else mate)],
            dst_ref=core_in.at[side],
            send_sem=d_send.at[side],
            recv_sem=d_recv.at[side],
            device_id={"dp": mate},
            device_id_type=MESH_ID,
        )

    def far_copy():
        return pltpu.make_async_remote_copy(
            src_ref=chip_sum,
            dst_ref=far_in,
            send_sem=d_send.at[2],
            recv_sem=d_recv.at[2],
            device_id={"dp": far},
            device_id_type=MESH_ID,
        )

    fill(far_mate)
    core_copy(0).start()
    fill(far)
    core_copy(0).wait_recv()

    def chip_add(n, carry):
        chip_sum[n] = (dsend[far * SLOTS + n] + core_in[0, n]).astype(jnp.bfloat16)
        return carry

    lax.fori_loop(0, SLOTS, chip_add, 0)
    far_copy().start()
    fill(mate)
    core_copy(1).start()
    fill(me)

    multiply(away, False, True)

    core_copy(1).wait_recv()
    far_copy().wait_recv()

    def add_up(n, carry):
        p = me * SLOTS + n
        dgrad_ref[0, n] = dsend[p] + core_in[1, n] + far_in[n].astype(jnp.float32)
        return carry

    lax.fori_loop(0, SLOTS, add_up, 0)
    core_copy(0).wait_send()
    core_copy(1).wait_send()
    far_copy().wait_send()
    for i in range(HALF):
        w_copy(me, HALF * grp + i, X).wait_send()
        w_copy(far, x_in(i), Y).wait_send()
    for ch in range(WCH):
        w_copy(me, ch, C_OWN).wait_send()
        w_copy(far, ch, C_FAR).wait_send()
    for shard in range(N_T):
        for ch in range(GCH):
            @pl.when((t > 0) & (shard >= t))
            def _():
                g_copy(shard, ch, 0).wait_send()

            @pl.when((t < N_T - 1) & (shard <= t))
            def _():
                g_copy(shard, ch, 1).wait_send()


def per_device_fused(
    attn_out, out_grad, base_weight, delta_values, block_rows, block_cols, block_owner
):
    smem = pl.BlockSpec(memory_space=pltpu.SMEM)
    hbm = pl.BlockSpec(memory_space=pl.ANY)
    dma = pltpu.SemaphoreType.DMA
    return tuple(pl.pallas_call(
        fused,
        out_shape=(
            pltpu.VMEM((TOK, WID), jnp.bfloat16),
            pltpu.VMEM((1, SLOTS, BS, BS), jnp.float32),
        ),
        in_specs=[smem, smem, smem, hbm, hbm, hbm, hbm],
        out_specs=(pl.BlockSpec(memory_space=pltpu.VMEM),) * 2,
        scratch_shapes=[
            pltpu.VMEM((N_DP, WID, WID), jnp.bfloat16),
            pltpu.VMEM((N_T * SPAN, TOK, BS), jnp.bfloat16),
            pltpu.VMEM((TOK, WID), jnp.float32),
            pltpu.VMEM((TOK, WID), jnp.bfloat16),
            pltpu.VMEM((SPAN, BS, TOK), jnp.bfloat16),
            pltpu.VMEM((N_DP * SLOTS, BS, BS), jnp.bfloat16),
            pltpu.VMEM((N_DP * SLOTS, BS, BS), jnp.float32),
            pltpu.VMEM((2, SLOTS, BS, BS), jnp.float32),
            pltpu.VMEM((SLOTS, BS, BS), jnp.bfloat16),
            pltpu.VMEM((SLOTS, BS, BS), jnp.bfloat16),
            pltpu.VMEM((5, SPAN, BS), jnp.int32),
            pltpu.SMEM((2, SPAN, BS), jnp.int32),
            pltpu.SMEM((3, SPAN, BS), jnp.int32),
            dma((2, N_T, GCH)),
            dma((N_T, GCH)),
            dma((4, WCH)),
            dma((N_DP, WCH)),
            dma((3,)),
            dma((3,)),
            dma((WCH + 7 + SPAN,)),
        ],
        compiler_params=pltpu.CompilerParams(
            collective_id=0, has_side_effects=True, vmem_limit_bytes=58 * 1024 * 1024
        ),
        cost_estimate=pl.CostEstimate(
            flops=2 * TOK * WID * D, bytes_accessed=16 * 1024 * 1024, transcendentals=0
        ),
    )(
        block_rows, block_cols, block_owner, attn_out, out_grad, base_weight, delta_values
    ))


def solution(mesh):
    placed = (
        P(("groups", "dp"), "tensor"),
        P(("groups", "dp"), "tensor"),
        P("tensor", "dp"),
        P("tensor", None, None),
        P("tensor"),
        P("tensor"),
        P("tensor"),
    )
    here = (mesh.shape["groups"], mesh.shape["dp"], mesh.shape["tensor"])
    return jax.shard_map(
        per_device_fused if here == (2, N_DP, N_T) else per_device,
        mesh=mesh,
        in_specs=placed,
        out_specs=(P(("groups", "dp"), "tensor"), P(("groups", "tensor"), "dp", None, None)),
        check_vma=False,
    )
```

```python
import jax
import jax.numpy as jnp
from jax import lax
from jax.experimental import pallas as pl
from jax.experimental.pallas import tpu as pltpu
from jax.sharding import PartitionSpec as P

D = 8192
BS = 128


def per_device(attn_out, out_grad, base_weight, delta_values, block_rows, block_cols, block_owner):
    tok_rows = attn_out.shape[0]
    feat_dev = attn_out.shape[1]
    row_span = feat_dev // BS
    col_span = base_weight.shape[1] // BS
    all_cols = D // BS
    dp_count = lax.axis_size("dp")
    dp_index = lax.axis_index("dp")
    piece_len = block_owner.shape[0]
    slot_cap = max(2, (piece_len + dp_count - 1) // dp_count)
    local_rows = block_rows % row_span
    local_cols = block_cols - dp_index * col_span
    row_pick = (local_rows[:, None] == jnp.arange(row_span, dtype=jnp.int32)[None, :]).astype(
        jnp.float32
    )
    col_pick = (local_cols[:, None] == jnp.arange(col_span, dtype=jnp.int32)[None, :]).astype(
        jnp.float32
    )
    added = jnp.einsum(
        "bx,by,brc->xryc",
        row_pick,
        col_pick,
        delta_values.astype(jnp.float32),
        precision=lax.Precision.HIGHEST,
    )
    w_eff = (base_weight.astype(jnp.float32) + added.reshape(feat_dev, col_span * BS)).astype(
        jnp.bfloat16
    )
    full_grad = lax.all_gather(out_grad, "tensor", axis=1, tiled=True)
    summed = lax.dot_general(
        full_grad,
        lax.all_gather(w_eff, "dp", axis=1, tiled=True),
        (((1,), (1,)), ((), ())),
        preferred_element_type=jnp.float32,
    )
    in_grad = summed.astype(jnp.bfloat16)
    left_sel = jnp.take(attn_out.reshape(tok_rows, row_span, BS), local_rows, axis=1)
    right_sel = jnp.take(full_grad.reshape(tok_rows, all_cols, BS), block_cols, axis=1)
    partial_blocks = jnp.einsum(
        "tbr,tbc->brc", left_sel, right_sel, preferred_element_type=jnp.float32
    )
    order = jnp.arange(piece_len, dtype=jnp.int32)
    same = block_owner[:, None] == block_owner[None, :]
    earlier = order[:, None] > order[None, :]
    slot = jnp.sum((same & earlier).astype(jnp.int32), axis=1)
    target = block_owner * slot_cap + slot
    places = jnp.arange(dp_count * slot_cap, dtype=jnp.int32)
    picker = (target[:, None] == places[None, :]).astype(jnp.float32)
    packed = jnp.einsum("bs,brc->src", picker, partial_blocks, precision=lax.Precision.HIGHEST)
    packed = packed.reshape(dp_count, slot_cap, BS, BS)
    received = lax.all_to_all(packed, "dp", split_axis=0, concat_axis=0, tiled=True)
    owned = jnp.sum(received, axis=0)
    return (in_grad, owned[None])


N_DP = 4
N_T = 4
SLOTS = 8
TOK = 512
WID = 2048
SPAN = WID // BS
GCH = 4
GBLK = SPAN // GCH
WCH = 8
HALF = WCH // 2
WROWS = WID // WCH
NT = 512
MESH_ID = pl.DeviceIdType.MESH


def fused(
    rows_ref, cols_ref, owner_ref, attn_hbm, grad_hbm, base_hbm, delta_hbm, out_ref, dgrad_ref,
    w_all, g_all, acc, attn, attn_t, delta, dsend, core_in,
    chip_sum, far_in, made, entry_ref, placed_ref,
    g_send, g_recv, w_send, w_recv, d_send, d_recv, loc,
):
    grp = lax.axis_index("groups")
    me = lax.axis_index("dp")
    t = lax.axis_index("tensor")
    core = me % 2
    mate = me + 1 - 2 * core
    far = (me + 2) % 4
    far_mate = (mate + 2) % 4

    barrier = pltpu.get_barrier_semaphore()
    for peer in (mate, far):
        pl.semaphore_signal(barrier, inc=1, device_id={"dp": peer}, device_id_type=MESH_ID)
    pl.semaphore_signal(barrier, inc=1, device_id={"groups": 1 - grp}, device_id_type=MESH_ID)

    @pl.when(t > 0)
    def _():
        pl.semaphore_signal(barrier, inc=1, device_id={"tensor": t - 1}, device_id_type=MESH_ID)

    @pl.when(t < N_T - 1)
    def _():
        pl.semaphore_signal(barrier, inc=1, device_id={"tensor": t + 1}, device_id_type=MESH_ID)

    def base_copy(ch):
        rows = pl.ds(pl.multiple_of(ch * WROWS, WROWS), WROWS)
        return pltpu.make_async_copy(base_hbm.at[rows], w_all.at[me, rows], loc.at[ch])

    def own_grad(b):
        cols = pl.ds(b * BS, BS)
        return pltpu.make_async_copy(
            grad_hbm.at[:, cols], g_all.at[t * SPAN + b], loc.at[WCH + 3 + b]
        )

    attn_copy = pltpu.make_async_copy(attn_hbm, attn, loc.at[WCH + 1])
    delta_copy = pltpu.make_async_copy(delta_hbm, delta, loc.at[WCH + 2])
    for b in range(SPAN):
        own_grad(b).start()
    delta_copy.start()
    for i in range(WCH):
        base_copy((HALF * grp + i) % WCH).start()
    attn_copy.start()

    last = N_T - 1
    pl.semaphore_wait(barrier, 3 + (t + last - 1) // last + (2 * last - 1 - t) // last)

    def g_copy(shard, ch, side):
        part = g_all.at[pl.ds(shard * SPAN + ch * GBLK, GBLK)]
        return pltpu.make_async_remote_copy(
            src_ref=part,
            dst_ref=part,
            send_sem=g_send.at[side, shard, ch],
            recv_sem=g_recv.at[shard, ch],
            device_id={"tensor": t - 1 if side == 0 else t + 1},
            device_id_type=MESH_ID,
        )

    for ch in range(GCH):
        for b in range(GBLK):
            own_grad(ch * GBLK + b).wait()

        @pl.when(t > 0)
        def _():
            g_copy(t, ch, 0).start()

        @pl.when(t < N_T - 1)
        def _():
            g_copy(t, ch, 1).start()

    X, Y, C_OWN, C_FAR = 0, 1, 2, 3

    def w_copy(shard, ch, kind):
        rows = pl.ds(pl.multiple_of(ch * WROWS, WROWS), WROWS)
        if kind == X:
            dev = {"dp": far}
        elif kind == Y:
            dev = {"groups": 1 - grp}
        else:
            dev = {"dp": mate}
        return pltpu.make_async_remote_copy(
            src_ref=w_all.at[shard, rows],
            dst_ref=w_all.at[shard, rows],
            send_sem=w_send.at[kind, ch],
            recv_sem=w_recv.at[shard, ch],
            device_id=dev,
            device_id_type=MESH_ID,
        )

    cell_row = lax.broadcasted_iota(jnp.int32, (SPAN, BS), 0)
    cell_col = lax.broadcasted_iota(jnp.int32, (SPAN, BS), 1) + me * SPAN
    place = lax.broadcasted_iota(jnp.int32, (SPAN, BS), 1)
    place_owner, place_slot = place >> 3, place & (SLOTS - 1)
    zero = jnp.zeros((SPAN, BS), jnp.int32)
    entry, entry_on, seen, row_at, col_at, on_at = zero, zero, zero, zero, zero, zero
    for n in range(rows_ref.shape[0]):
        row, col, owner = rows_ref[n] & (SPAN - 1), cols_ref[n], owner_ref[n]
        hit = (cell_row == row) & (cell_col == col)
        entry = jnp.where(hit, n, entry)
        entry_on = jnp.where(hit, 1, entry_on)
        mine = place_owner == owner
        fits = mine & (place_slot == seen)
        row_at = jnp.where(fits, row, row_at)
        col_at = jnp.where(fits, col, col_at)
        on_at = jnp.where(fits, 1, on_at)
        seen = jnp.where(mine, seen + 1, seen)
    for n, table in enumerate((entry, entry_on, row_at, col_at, on_at)):
        made[n] = table
    entry_copy = pltpu.make_async_copy(made.at[pl.ds(0, 2)], entry_ref, loc.at[WCH + 5 + SPAN])
    placed_copy = pltpu.make_async_copy(made.at[pl.ds(2, 3)], placed_ref, loc.at[WCH + 6 + SPAN])
    entry_copy.start()
    placed_copy.start()
    entry_copy.wait()
    placed_copy.wait()

    delta_copy.wait()
    for i in range(WCH):
        ch = (HALF * grp + i) % WCH
        base_copy(ch).wait()

        def add_cell(n, carry, ch=ch):
            r, c = n // SPAN, n % SPAN
            rows = pl.ds(pl.multiple_of(ch * WROWS + r * BS, BS), BS)
            cols = pl.ds(pl.multiple_of(c * BS, BS), BS)
            at = ch * (WROWS // BS) + r
            extra = delta[entry_ref[0, at, c]].astype(jnp.float32)
            extra = extra * entry_ref[1, at, c].astype(jnp.float32)
            w_all[me, rows, cols] = (w_all[me, rows, cols].astype(jnp.float32) + extra).astype(
                jnp.bfloat16
            )
            return carry

        lax.fori_loop(0, WROWS // BS * SPAN, add_cell, 0)
        if i < HALF:
            w_copy(me, ch, X).start()
        w_copy(me, ch, C_OWN).start()

    attn_copy.wait()

    def flip(r, carry):
        cols = pl.ds(pl.multiple_of(r * BS, BS), BS)
        attn_t[r] = attn[:, cols].T
        return carry

    lax.fori_loop(0, SPAN, flip, 0)

    def left_in(m):
        return t - 1 - m // GCH, m % GCH

    def right_in(m):
        return t + 1 + m // GCH, m % GCH

    def take_left(m):
        shard, ch = left_in(m)

        @pl.when(shard >= 0)
        def _():
            g_copy(shard, ch, 1).wait_recv()

            @pl.when(t < N_T - 1)
            def _():
                g_copy(shard, ch, 1).start()

    def take_right(m):
        shard, ch = right_in(m)

        @pl.when(shard < N_T)
        def _():
            g_copy(shard, ch, 0).wait_recv()

            @pl.when(t > 0)
            def _():
                g_copy(shard, ch, 0).start()

    def x_in(i):
        return HALF * grp + i

    def y_in(i):
        return HALF * (1 - grp) + i

    for r in range(5):
        if r < 4:
            for m in range(r * GCH // 2, (r + 1) * GCH // 2):
                take_left(m)
                take_right(m)
            w_copy(far, x_in(r), X).wait_recv()
            w_copy(far, x_in(r), Y).start()
            w_copy(far, x_in(r), C_FAR).start()
        if r >= 1:
            w_copy(far, y_in(r - 1), Y).wait_recv()
            w_copy(far, y_in(r - 1), C_FAR).start()

    for ch in range(WCH):
        w_copy(mate, ch, C_OWN).wait_recv()
    for ch in range(WCH):
        w_copy(far_mate, ch, C_FAR).wait_recv()

    def multiply(shard, first, last):
        def tile(n, carry):
            cols = pl.ds(pl.multiple_of(n * NT, NT), NT)
            left = jnp.concatenate([g_all[shard * SPAN + b] for b in range(SPAN)], axis=1)
            part = lax.dot_general(
                left, w_all[shard, cols, :], (((1,), (1,)), ((), ())),
                preferred_element_type=jnp.float32,
            )
            if first:
                acc[:, cols] = part
            elif last:
                out_ref[:, cols] = (acc[:, cols] + part).astype(jnp.bfloat16)
            else:
                acc[:, cols] += part
            return carry

        lax.fori_loop(0, WID // NT, tile, 0)

    away = jnp.where(t < N_T // 2, N_T - 1, 0)
    toward = jnp.where(t < N_T // 2, 1, -1)
    multiply((away + toward) % N_T, True, False)
    multiply((away + 2 * toward) % N_T, False, False)
    multiply((away + 3 * toward) % N_T, False, False)
    for m in range(2 * GCH, 3 * GCH):
        take_left(m)
        take_right(m)

    def fill(peer):
        def one_place(n, carry):
            p = peer * SLOTS + n
            block = jnp.dot(
                attn_t[placed_ref[0, 0, p]], g_all[placed_ref[1, 0, p]],
                preferred_element_type=jnp.float32,
            )
            dsend[p] = block * placed_ref[2, 0, p].astype(jnp.float32)
            return carry

        lax.fori_loop(0, SLOTS, one_place, 0, unroll=8)

    def slots_of(peer):
        return pl.ds(pl.multiple_of(peer * SLOTS, SLOTS), SLOTS)

    def core_copy(side):
        return pltpu.make_async_remote_copy(
            src_ref=dsend.at[slots_of(far_mate if side == 0 else mate)],
            dst_ref=core_in.at[side],
            send_sem=d_send.at[side],
            recv_sem=d_recv.at[side],
            device_id={"dp": mate},
            device_id_type=MESH_ID,
        )

    def far_copy():
        return pltpu.make_async_remote_copy(
            src_ref=chip_sum,
            dst_ref=far_in,
            send_sem=d_send.at[2],
            recv_sem=d_recv.at[2],
            device_id={"dp": far},
            device_id_type=MESH_ID,
        )

    fill(far_mate)
    core_copy(0).start()
    fill(far)
    core_copy(0).wait_recv()

    def chip_add(n, carry):
        chip_sum[n] = (dsend[far * SLOTS + n] + core_in[0, n]).astype(jnp.bfloat16)
        return carry

    lax.fori_loop(0, SLOTS, chip_add, 0)
    far_copy().start()
    fill(mate)
    core_copy(1).start()
    fill(me)

    multiply(away, False, True)

    core_copy(1).wait_recv()
    far_copy().wait_recv()

    def add_up(n, carry):
        p = me * SLOTS + n
        dgrad_ref[0, n] = dsend[p] + core_in[1, n] + far_in[n].astype(jnp.float32)
        return carry

    lax.fori_loop(0, SLOTS, add_up, 0)
    core_copy(0).wait_send()
    core_copy(1).wait_send()
    far_copy().wait_send()
    for i in range(HALF):
        w_copy(me, HALF * grp + i, X).wait_send()
        w_copy(far, x_in(i), Y).wait_send()
    for ch in range(WCH):
        w_copy(me, ch, C_OWN).wait_send()
        w_copy(far, ch, C_FAR).wait_send()
    for shard in range(N_T):
        for ch in range(GCH):
            @pl.when((t > 0) & (shard >= t))
            def _():
                g_copy(shard, ch, 0).wait_send()

            @pl.when((t < N_T - 1) & (shard <= t))
            def _():
                g_copy(shard, ch, 1).wait_send()


def per_device_fused(
    attn_out, out_grad, base_weight, delta_values, block_rows, block_cols, block_owner
):
    smem = pl.BlockSpec(memory_space=pltpu.SMEM)
    hbm = pl.BlockSpec(memory_space=pl.ANY)
    dma = pltpu.SemaphoreType.DMA
    return tuple(pl.pallas_call(
        fused,
        out_shape=(
            pltpu.VMEM((TOK, WID), jnp.bfloat16),
            pltpu.VMEM((1, SLOTS, BS, BS), jnp.float32),
        ),
        in_specs=[smem, smem, smem, hbm, hbm, hbm, hbm],
        out_specs=(pl.BlockSpec(memory_space=pltpu.VMEM),) * 2,
        scratch_shapes=[
            pltpu.VMEM((N_DP, WID, WID), jnp.bfloat16),
            pltpu.VMEM((N_T * SPAN, TOK, BS), jnp.bfloat16),
            pltpu.VMEM((TOK, WID), jnp.float32),
            pltpu.VMEM((TOK, WID), jnp.bfloat16),
            pltpu.VMEM((SPAN, BS, TOK), jnp.bfloat16),
            pltpu.VMEM((N_DP * SLOTS, BS, BS), jnp.bfloat16),
            pltpu.VMEM((N_DP * SLOTS, BS, BS), jnp.float32),
            pltpu.VMEM((2, SLOTS, BS, BS), jnp.float32),
            pltpu.VMEM((SLOTS, BS, BS), jnp.bfloat16),
            pltpu.VMEM((SLOTS, BS, BS), jnp.bfloat16),
            pltpu.VMEM((5, SPAN, BS), jnp.int32),
            pltpu.SMEM((2, SPAN, BS), jnp.int32),
            pltpu.SMEM((3, SPAN, BS), jnp.int32),
            dma((2, N_T, GCH)),
            dma((N_T, GCH)),
            dma((4, WCH)),
            dma((N_DP, WCH)),
            dma((3,)),
            dma((3,)),
            dma((WCH + 7 + SPAN,)),
        ],
        compiler_params=pltpu.CompilerParams(
            collective_id=0, has_side_effects=True, vmem_limit_bytes=58 * 1024 * 1024
        ),
        cost_estimate=pl.CostEstimate(
            flops=2 * TOK * WID * D, bytes_accessed=16 * 1024 * 1024, transcendentals=0
        ),
    )(
        block_rows, block_cols, block_owner, attn_out, out_grad, base_weight, delta_values
    ))


def solution(mesh):
    placed = (
        P(("groups", "dp"), "tensor"),
        P(("groups", "dp"), "tensor"),
        P("tensor", "dp"),
        P("tensor", None, None),
        P("tensor"),
        P("tensor"),
        P("tensor"),
    )
    here = (mesh.shape["groups"], mesh.shape["dp"], mesh.shape["tensor"])
    return jax.shard_map(
        per_device_fused if here == (2, N_DP, N_T) else per_device,
        mesh=mesh,
        in_specs=placed,
        out_specs=(P(("groups", "dp"), "tensor"), P(("groups", "tensor"), "dp", None, None)),
        check_vma=False,
    )
```
